128 devices in a mesh: blk: 4 (over x), pts: 32 (over y, z, core).
Axes of the slice: x: 4, y: 4, z: 4, core: 2. Of those that a mesh axis runs over, the one named last changes fastest.
Arguments:
- snapshots: bfloat16 [4096, 3, 65536], P('blk', None, 'pts'), may hold values from -6 to 6
- tail_rows: bfloat16 [128, 3, 65536], P(None, None, 'pts'), may hold values from -6 to 6
- point_weight: float32 [3, 65536], P(None, 'pts'), may hold values from 0.2 to 2
- freq_bins: int32 [16], replicated, may hold values from 1 to 127
Outputs:
- recon: bfloat16 [16, 2, 32, 3, 65536], P('blk', None, None, None, 'pts')
The draws below stay inside these ranges and needn't reach their ends.
All inputs are finite; a program needn't handle non-finite values.
Results may differ from the reference program's by a relative error of at most 0.0067.
Values may be sent and summed in bfloat16 or wider, within the bound.
No kernel may reach another device: no remote copies, remote signals or barrier semaphores. Data moves between devices by JAX's collectives and lax.ppermute only.
A program may use at most 192 MiB of HBM per device.

```python
import math
import jax
import jax.numpy as jnp
from jax import lax

NFFT = 256
NF = 16
MODES = 4
EIG_ITERS = 3
HALF = 128
NB = 32
SNAPS = 4096
GRID = 65536


def set_ends(array, stream_key, low, largest):
    longest = array.shape.index(max(array.shape))
    spots = []
    for shift in (0, 1):
        where = [jax.random.randint(jax.random.fold_in(stream_key, axis), (), 0, length) for axis, length in enumerate(array.shape)]
        where[longest] = (where[longest] + shift) % array.shape[longest]
        spots.append(tuple(where))
    return array.at[spots[0]].set(low).at[spots[1]].set(largest)


def levels(own_key, dims, shards, least, largest):
    def one(position, parts):
        draws = jax.random.uniform(jax.random.fold_in(jax.random.fold_in(own_key, 6), position), (parts,), jnp.float32, least / len(shards), largest / len(shards))
        return jnp.repeat(jnp.exp(draws), dims[position] // parts).reshape((-1,) + (1,) * (len(dims) - position - 1))

    factor_of = one(*shards[0])
    for cut in shards[1:]:
        factor_of = factor_of * one(*cut)
    return factor_of


def normal_values(rng, shape, spread, limit, shards=(), kind=jnp.bfloat16):
    values = jax.random.normal(rng, shape, jnp.float32) * spread
    if len(shards) > 0:
        values = levels(rng, shape, shards, -0.22, 0.18) * values
    return jnp.clip(values, min=-limit, max=limit).astype(kind)


def setup_inputs(seed: int = 0) -> dict:
    key_of = jax.random.split(jax.random.key(seed), 5)
    snapshots = normal_values(key_of[0], (SNAPS, 3, GRID), 1.0, 6.0, ((0, 4), (2, 32)))
    tail_rows = normal_values(key_of[1], (HALF, 3, GRID), 1.0, 6.0, ((2, 32),))
    point_weight = jnp.clip(jnp.exp(math.log(2.0) - 2.3025851 * jax.random.uniform(key_of[2], (3, GRID), jnp.float32) ** levels(key_of[2], (3, GRID), ((1, 32),), -0.2, 0.2)), 0.2, 2.0)
    freq_bins = set_ends(jax.random.randint(key_of[3], (NF,), 1, NFFT // 2), jax.random.fold_in(key_of[3], 1), 1, (NFFT // 2) - 1).astype(jnp.int32)
    return dict(snapshots=snapshots, tail_rows=tail_rows, point_weight=point_weight, freq_bins=freq_bins)


def fourier_table(freq_bins, length):
    steps = jnp.arange(length, dtype=jnp.int32)
    product = freq_bins[:, None] * steps[None, :] % length
    angle = product.astype(jnp.float32) * (2.0 * math.pi / length)
    window = 0.5 - 0.5 * jnp.cos(steps.astype(jnp.float32) * (2.0 * math.pi / length))
    cosine = window[None, :] * jnp.cos(angle)
    sine = -window[None, :] * jnp.sin(angle)
    return jnp.concatenate([cosine, sine], axis=0).astype(jnp.bfloat16)

def weighted_gram(side_rows, weight):
    values = side_rows.astype(jnp.float32)
    return jnp.dot(values * weight[None, :], values.T, precision=lax.Precision.HIGHEST)

def spectral(gram_matrix, blocks):
    real_part = gram_matrix[:blocks, :blocks] + gram_matrix[blocks:, blocks:]
    imag_part = gram_matrix[:blocks, blocks:] - gram_matrix[blocks:, :blocks]
    upper = jnp.concatenate([real_part, imag_part], axis=1)
    lower = jnp.concatenate([-imag_part, real_part], axis=1)
    return jnp.concatenate([upper, lower], axis=0)

def orthonormal(basis):
    inner = jnp.dot(basis.T, basis, precision=lax.Precision.HIGHEST)
    factor = jnp.linalg.cholesky(inner)
    return lax.linalg.triangular_solve(factor, basis, left_side=False, lower=True, transpose_a=True)

def projector(operator, blocks):
    basis = jnp.concatenate([operator[:, :MODES], operator[:, blocks:blocks + MODES]], axis=1)
    basis = orthonormal(basis)
    for sweep in range(EIG_ITERS):
        basis = orthonormal(jnp.dot(operator, basis, precision=lax.Precision.HIGHEST))
    return jnp.dot(basis, basis.T, precision=lax.Precision.HIGHEST)

def reference(snapshots, tail_rows, point_weight, freq_bins):
    series = jnp.concatenate([snapshots, tail_rows], axis=0).reshape(SNAPS + HALF, 3 * GRID)
    table = fourier_table(freq_bins, NFFT)
    weight = point_weight.reshape(-1)
    pieces = []
    for block_index in range(NB):
        window_rows = series[block_index * HALF:block_index * HALF + NFFT]
        pieces.append(jnp.dot(table.astype(jnp.float32), window_rows.astype(jnp.float32), preferred_element_type=jnp.float32).astype(jnp.bfloat16))
    coefficients = jnp.stack(pieces, axis=1)
    results = []
    for freq_index in range(NF):
        side_rows = jnp.concatenate([coefficients[freq_index], coefficients[NF + freq_index]], axis=0)
        cross_gram = weighted_gram(side_rows, weight)
        projection = projector(spectral(cross_gram, NB), NB).astype(jnp.bfloat16)
        filtered = jnp.dot(projection.astype(jnp.float32), side_rows.astype(jnp.float32), preferred_element_type=jnp.float32).astype(jnp.bfloat16)
        results.append(filtered.reshape(2, NB, 3, GRID))
    return jnp.stack(results, axis=0)
```

```python
import functools
import math

import jax
import jax.numpy as jnp
from jax import lax
from jax.experimental import pallas as pl
from jax.experimental.pallas import tpu as pltpu
from jax.sharding import PartitionSpec as P

MODES = 4
EIG_ITERS = 3
TILE = 512
CHUNKS = (1, 3, 4, 3, 1)
HIGHEST = lax.Precision.HIGHEST


def fourier_table(freq_bins, length):
    steps = jnp.arange(length, dtype=jnp.int32)
    product = freq_bins[:, None] * steps[None, :] % length
    angle = product.astype(jnp.float32) * (2.0 * math.pi / length)
    window = 0.5 - 0.5 * jnp.cos(steps.astype(jnp.float32) * (2.0 * math.pi / length))
    cosine = window[None, :] * jnp.cos(angle)
    sine = -window[None, :] * jnp.sin(angle)
    table = jnp.stack([cosine, sine], axis=1).astype(jnp.bfloat16)
    return table.reshape(2 * freq_bins.shape[0], length)


def banded(table, blocks):
    rows, length = table.shape
    half = length // 2
    block = lax.broadcasted_iota(jnp.int32, (rows, blocks, blocks, half), 1)
    part = lax.broadcasted_iota(jnp.int32, (rows, blocks, blocks, half), 2)
    first = table[:, None, None, :half]
    second = table[:, None, None, half:]
    zero = jnp.zeros((), table.dtype)
    full = jnp.where(part == block, first, jnp.where(part == block + 1, second, zero))
    return full.reshape(rows * blocks, blocks * half)


def fourier_kernel(me_ref, band_ref, edge_ref, x_ref, tail_ref, *outs):
    main = jnp.dot(band_ref[...], x_ref[0], preferred_element_type=jnp.float32)
    main = main.astype(jnp.bfloat16)
    size = main.shape[0] // len(outs)
    half = tail_ref.shape[1]
    for peer, out in enumerate(outs):
        out[:size, :] = main[peer * size : (peer + 1) * size]

    def edge(rows):
        result = jnp.dot(edge_ref[...], rows, preferred_element_type=jnp.float32)
        result = result.astype(jnp.bfloat16)
        step = result.shape[0] // len(outs)
        for peer, out in enumerate(outs):
            out[size:, :] = result[peer * step : (peer + 1) * step]

    @pl.when(me_ref[0] == 0)
    def _():
        edge(tail_ref[0])

    @pl.when(me_ref[0] != 0)
    def _():
        edge(x_ref[0, :half, :])


def fourier(me, band, edge, snapshots, tail, first_tile, tiles):
    comps, rows, points = snapshots.shape
    half = tail.shape[1]
    per_comp = points // TILE
    size = band.shape[0] // 4 + edge.shape[0] // 4

    def place(t):
        return ((t + first_tile) // per_comp, 0, (t + first_tile) % per_comp)

    return pl.pallas_call(
        fourier_kernel,
        grid=(tiles,),
        in_specs=[
            pl.BlockSpec(memory_space=pltpu.SMEM),
            pl.BlockSpec(band.shape, lambda t: (0, 0)),
            pl.BlockSpec(edge.shape, lambda t: (0, 0)),
            pl.BlockSpec((1, rows, TILE), place),
            pl.BlockSpec((1, half, TILE), place),
        ],
        out_specs=[pl.BlockSpec((size, TILE), lambda t: (0, t))] * 4,
        out_shape=[jax.ShapeDtypeStruct((size, tiles * TILE), jnp.bfloat16)] * 4,
        compiler_params=pltpu.CompilerParams(vmem_limit_bytes=48 * 2**20),
        cost_estimate=pl.CostEstimate(
            flops=2 * band.shape[0] * rows * tiles * TILE,
            bytes_accessed=2 * (rows + half + 4 * size) * tiles * TILE,
            transcendentals=0,
        ),
        name="fourier",
    )(me, band, edge, snapshots, tail)


def gram_kernel(me_ref, weight_ref, *refs):
    parts, refs = refs[:4], refs[4:]
    total_in = refs[0] if len(refs) == 5 else None
    total_ref, side_ref, total = refs[-3:]
    step = pl.program_id(0)
    me = me_ref[0]

    @pl.when(step == 0)
    def _():
        total[...] = jnp.zeros_like(total)

    last = lax.broadcasted_iota(jnp.int32, (8, TILE), 0) == 7
    for peer in range(4):
        group = lax.rem(me - peer + 4, 4)
        rows = parts[peer][:64, :].astype(jnp.float32)
        edge = parts[(peer - 1) % 4][64:72, :].astype(jnp.float32)
        pieces = [
            rows[8 * k : 8 * k + 8] + jnp.where(last, edge[k : k + 1], 0.0) for k in range(8)
        ]
        for freq in range(4):
            both = jnp.concatenate(pieces[2 * freq : 2 * freq + 2], axis=0)
            start = pl.multiple_of(64 * freq + 16 * group, 16)
            side_ref[pl.ds(start, 16), :] = both.astype(jnp.bfloat16)
    side = side_ref[...]
    scaled = side.astype(jnp.float32) * weight_ref[...]
    high = scaled.astype(jnp.bfloat16)
    low = (scaled - high.astype(jnp.float32)).astype(jnp.bfloat16)
    dims = (((1,), (1,)), ((), ()))
    total[...] += lax.dot_general(
        high, side, dims, preferred_element_type=jnp.float32
    ) + lax.dot_general(low, side, dims, preferred_element_type=jnp.float32)

    @pl.when(step == pl.num_programs(0) - 1)
    def _():
        lane = lax.broadcasted_iota(jnp.int32, (8, 128), 1)
        real_lane = lax.rem(lane, 16) < 8
        low_lane = lane < 64
        for pair in range(2):
            for group in range(4):
                tops = []
                for freq in (2 * pair, 2 * pair + 1):
                    start = 64 * freq + 16 * group
                    columns = slice(128 * pair, 128 * pair + 128)
                    real = total[start : start + 8, columns]
                    imag = total[start + 8 : start + 16, columns]
                    turned = jnp.where(
                        real_lane, pltpu.roll(imag, 120, 1), -pltpu.roll(imag, 8, 1)
                    )
                    tops.append(real + turned)
                rows = slice(32 * pair + 8 * group, 32 * pair + 8 * group + 8)
                top = jnp.where(low_lane, tops[0], tops[1])
                total_ref[rows, :] = top if total_in is None else top + total_in[rows, :]


def gram(me, weight, parts, before, first_tile, tiles):
    size = parts[0].shape[0]
    width = weight.shape[1]
    before_specs = [pl.BlockSpec((64, 128), lambda t: (0, 0)), pl.BlockSpec(memory_space=pl.ANY)]
    return pl.pallas_call(
        gram_kernel,
        grid=(tiles,),
        in_specs=[
            pl.BlockSpec(memory_space=pltpu.SMEM),
            pl.BlockSpec((1, TILE), lambda t: (0, t + first_tile)),
        ]
        + [pl.BlockSpec((size, TILE), lambda t: (0, t))] * 4
        + before_specs[: len(before)],
        out_specs=[
            pl.BlockSpec((64, 128), lambda t: (0, 0)),
            pl.BlockSpec((256, TILE), lambda t: (0, t + first_tile)),
        ],
        out_shape=[
            jax.ShapeDtypeStruct((64, 128), jnp.float32),
            jax.ShapeDtypeStruct((256, width), jnp.bfloat16),
        ],
        scratch_shapes=[pltpu.VMEM((256, 256), jnp.float32)],
        input_output_aliases={7: 1} if before else {},
        compiler_params=pltpu.CompilerParams(vmem_limit_bytes=32 * 2**20),
        cost_estimate=pl.CostEstimate(
            flops=4 * 256 * 256 * tiles * TILE,
            bytes_accessed=2 * (4 * size + 256) * tiles * TILE,
            transcendentals=0,
        ),
        name="gram",
    )(me, weight, *parts, *before)


def projections(total_ref, proj_ref):
    lane = lax.broadcasted_iota(jnp.int32, (8, 128), 1)
    row = lax.broadcasted_iota(jnp.int32, (8, 128), 0)
    real_lane = lax.rem(lane, 16) < 8
    low_lane = lane < 64
    low_row = row < 4
    own_lane = low_row == low_lane
    place = lax.rem(row, 4)

    def turn(value):
        return jnp.where(real_lane, -pltpu.roll(value, 120, 1), pltpu.roll(value, 8, 1))

    def pick(value, j):
        return jnp.where(low_row, value[j : j + 1], value[4 + j : 5 + j])

    def orthonormal(base):
        other = turn(base)
        for j in range(MODES):
            one, two = pick(base, j), pick(other, j)
            along = jnp.sum(base * one, axis=1, keepdims=True)
            across = jnp.sum(base * two, axis=1, keepdims=True)
            norm = pick(along, j)
            inverse = 1.0 / norm
            a, b = along * inverse, across * inverse
            scale = lax.rsqrt(norm)
            later = place > j
            new_base = jnp.where(later, base - a * one - b * two, base)
            new_other = jnp.where(later, other - a * two + b * one, other)
            here = place == j
            base = jnp.where(here, base * scale, new_base)
            other = jnp.where(here, other * scale, new_other)
        return base, other

    for pair in range(2):
        blocks = [total_ref[32 * pair + 8 * g : 32 * pair + 8 * g + 8, :] for g in range(4)]
        operator = []
        for keep in (low_lane, jnp.logical_not(low_lane)):
            for block in blocks:
                top = jnp.where(keep, block, 0.0)
                operator += [top, turn(top)]
        operator = jnp.concatenate(operator, axis=0)
        first = blocks[0]
        base = jnp.where(low_row, first, pltpu.roll(first, 4, 0))
        base = jnp.where(own_lane, base, 0.0)
        base, other = orthonormal(base)
        for sweep in range(EIG_ITERS):
            base = jnp.dot(base, operator, precision=HIGHEST, preferred_element_type=jnp.float32)
            base, other = orthonormal(base)
        both = jnp.concatenate([base, other], axis=0)
        whole = lax.dot_general(
            both, both, (((0,), (0,)), ((), ())), precision=HIGHEST,
            preferred_element_type=jnp.float32,
        )
        rows = []
        for freq in range(2):
            for part in range(2):
                for group in range(4):
                    start = 64 * freq + 16 * group + 8 * part
                    rows.append(whole[start : start + 8])
        proj_ref[pair] = jnp.concatenate(rows, axis=0).astype(jnp.bfloat16)


def recon_kernel(total_ref, side_ref, out_ref, proj_ref):
    @pl.when(pl.program_id(0) == 0)
    def _():
        projections(total_ref, proj_ref)

    for pair in range(2):
        result = jnp.dot(
            proj_ref[pair],
            side_ref[128 * pair : 128 * pair + 128, :],
            preferred_element_type=jnp.float32,
        ).astype(jnp.bfloat16)
        for freq in range(2):
            for part in range(2):
                start = 64 * freq + 32 * part
                out_ref[2 * pair + freq, part, 0] = result[start : start + 32]


def recon(total, side, comps, points):
    tile = 1024
    per_comp = points // tile
    return pl.pallas_call(
        recon_kernel,
        grid=(comps * per_comp,),
        in_specs=[
            pl.BlockSpec(total.shape, lambda t: (0, 0)),
            pl.BlockSpec((256, tile), lambda t: (0, t)),
        ],
        out_specs=pl.BlockSpec(
            (4, 2, 1, 32, tile), lambda t: (0, 0, t // per_comp, 0, t % per_comp)
        ),
        out_shape=jax.ShapeDtypeStruct((4, 2, comps, 32, points), jnp.bfloat16),
        scratch_shapes=[pltpu.VMEM((2, 128, 128), jnp.bfloat16)],
        compiler_params=pltpu.CompilerParams(vmem_limit_bytes=32 * 2**20),
        name="recon",
    )(total, side)


def point_sum(value):
    def moved(array, dy, dz, dc):
        def index(y, z, c):
            return (y % 4) * 8 + (z % 4) * 2 + c % 2

        pairs = [
            (index(y, z, c), index(y + dy, z + dz, c + dc))
            for y in range(4)
            for z in range(4)
            for c in range(2)
        ]
        return lax.ppermute(array, "pts", pairs)

    value = value + moved(value, 0, 0, 1)
    value = value + moved(value, 0, 1, 0) + moved(value, 0, -1, 0) + moved(value, 0, 2, 0)
    return value + moved(value, 1, 0, 0) + moved(value, -1, 0, 0) + moved(value, 2, 0, 0)


def on_device(snapshots, tail_rows, point_weight, freq_bins):
    row_count, comps, points = snapshots.shape
    half = tail_rows.shape[0]
    snapshots = jnp.transpose(snapshots, (1, 0, 2))
    tail = jnp.transpose(tail_rows, (1, 0, 2))
    weight = point_weight.reshape(1, comps * points)
    position = lax.axis_index("blk")
    me = position.astype(jnp.int32).reshape(1)
    freq_count = freq_bins.shape[0]
    own = freq_count // 4
    turned = lax.dynamic_slice(jnp.concatenate([freq_bins, freq_bins]), (own * position,), (freq_count,))
    table = fourier_table(turned, 2 * half)
    band = banded(table, row_count // half)
    edge = table[:, half:]
    arrived = []
    starts = [sum(CHUNKS[:k]) for k in range(len(CHUNKS))]
    for start, tiles in zip(starts, CHUNKS):
        sent = fourier(me, band, edge, snapshots, tail, start, tiles)
        parts = [sent[0]]
        for shift in range(1, 4):
            pairs = [(k, (k + shift) % 4) for k in range(4)]
            parts.append(lax.ppermute(sent[shift], "blk", pairs))
        arrived.append(parts)
    before = ()
    for start, tiles, parts in zip(starts, CHUNKS, arrived):
        before = gram(me, weight, parts, before, start, tiles)
    total, side = before
    total = point_sum(total)
    out = recon(total, side, comps, points)
    return jnp.transpose(out, (0, 1, 3, 2, 4))


def solution(mesh):
    in_specs = (P("blk", None, "pts"), P(None, None, "pts"), P(None, "pts"), P())
    out_specs = P("blk", None, None, None, "pts")
    return jax.shard_map(
        on_device, mesh=mesh, in_specs=in_specs, out_specs=out_specs, check_vma=False
    )
```

```python
import functools
import math

import jax
import jax.numpy as jnp
from jax import lax
from jax.experimental import pallas as pl
from jax.experimental.pallas import tpu as pltpu
from jax.sharding import PartitionSpec as P

MODES = 4
EIG_ITERS = 3
TILE = 512
CHUNKS = (2048, 2048, 1536, 512)
COST = 1000000


def pieces(start, width, points, most):
    result = []
    at = 0
    while at < width:
        column = (start + at) % points
        size = min(most, width - at, points - column)
        result.append((at, (start + at) // points, column, size))
        at += size
    return result


def band_kernel(me_ref, freq_ref, x_ref, tail_ref, *refs, parts):
    outs, refs = refs[:4], refs[4:]
    band_ref, edge_ref, freqs, table_ref, freq_sem = refs[:5]
    fetches = start_fetches(me_ref, x_ref, tail_ref, refs[5:], parts)
    fetch = pltpu.make_async_copy(freq_ref, freqs, freq_sem)
    fetch.start()
    fetch.wait()
    me = me_ref[0]
    half = edge_ref.shape[1]
    length = 2 * half
    row = lax.broadcasted_iota(jnp.int32, (32, length), 0)
    steps = lax.broadcasted_iota(jnp.int32, (32, length), 1)
    bins = jnp.zeros((32, length), jnp.int32)
    for k in range(16):
        bins = jnp.where(row // 2 == k, freqs[lax.rem(4 * me + k, 16)], bins)
    turns = (bins * steps + (length // 4) * lax.rem(row, 2)) & (length - 1)
    window = 0.5 - 0.5 * jnp.cos(steps[:1].astype(jnp.float32) * (2.0 * math.pi / length))
    table = window * jnp.cos(turns.astype(jnp.float32) * (2.0 * math.pi / length))
    table_ref[...] = table
    edge_ref[...] = table[:, half:].astype(jnp.bfloat16)
    block = lax.broadcasted_iota(jnp.int32, (8, half), 0)
    for r in range(0, 32, 2):
        for part in range(8):
            rows = []
            for one in (r, r + 1):
                value = jnp.where(block == part, table_ref[one : one + 1, :half], 0.0)
                rows.append(jnp.where(block == part - 1, table_ref[one : one + 1, half:], value))
            band_ref[8 * r : 8 * r + 16, half * part : half * part + half] = jnp.concatenate(
                rows, axis=0
            ).astype(jnp.bfloat16)
    transform(me_ref, band_ref, edge_ref, outs, refs[5:], parts, fetches)


def fourier_kernel(me_ref, band_ref, edge_ref, x_ref, tail_ref, *refs, parts):
    outs, refs = refs[:4], refs[4:]
    fetches = start_fetches(me_ref, x_ref, tail_ref, refs[1:], parts)
    refs[0][0] = me_ref[0]
    transform(me_ref, band_ref, edge_ref, outs, refs[1:], parts, fetches)


def start_fetches(me_ref, x_ref, tail_ref, scratch, parts):
    held, tails, sems, tail_sems = scratch
    fetches = []
    for k, (at, comp, column, size) in enumerate(parts):
        source, here = pl.ds(column, size), pl.ds(at, size)
        fetches.append(
            (
                pltpu.make_async_copy(x_ref.at[comp, :, source], held.at[:, here], sems.at[k]),
                pltpu.make_async_copy(
                    tail_ref.at[comp, :, source], tails.at[:, here], tail_sems.at[k]
                ),
            )
        )
    for fetch, _ in fetches:
        fetch.start()

    @pl.when(me_ref[0] == 0)
    def _():
        for _, fetch_tail in fetches:
            fetch_tail.start()

    return fetches


def transform(me_ref, band_ref, edge_ref, outs, scratch, parts, fetches):
    held, tails = scratch[:2]
    half = tails.shape[0]

    def edge(rows, here):
        result = jnp.dot(edge_ref[...], rows, preferred_element_type=jnp.float32)
        result = result.astype(jnp.bfloat16)
        for peer, out in enumerate(outs):
            out[64:, here] = result[8 * peer : 8 * peer + 8]

    for (at, _, _, size), (fetch, fetch_tail) in zip(parts, fetches):
        here = slice(at, at + size)
        fetch.wait()
        main = jnp.dot(band_ref[...], held[:, here], preferred_element_type=jnp.float32)
        main = main.astype(jnp.bfloat16)
        for peer, out in enumerate(outs):
            out[:64, here] = main[64 * peer : 64 * peer + 64]

        @pl.when(me_ref[0] == 0)
        def _():
            fetch_tail.wait()
            edge(tails[:, here], here)

        @pl.when(me_ref[0] != 0)
        def _():
            edge(held[:half, here], here)


def fourier(me, freq_bins, band, edge, snapshots, tail, start, width):
    comps, rows, points = snapshots.shape
    half = tail.shape[1]
    parts = pieces(start, width, points, TILE)
    vmem = pl.BlockSpec(memory_space=pltpu.VMEM)
    smem = pl.BlockSpec(memory_space=pltpu.SMEM)
    hbm = pl.BlockSpec(memory_space=pl.ANY)
    out_shape = [jax.ShapeDtypeStruct((72, width), jnp.bfloat16)] * 4
    scratch = [
        pltpu.VMEM((rows, width), jnp.bfloat16),
        pltpu.VMEM((half, width), jnp.bfloat16),
        pltpu.SemaphoreType.DMA((len(parts),)),
        pltpu.SemaphoreType.DMA((len(parts),)),
    ]
    if band is None:
        kernel, operands, in_specs = band_kernel, (me, freq_bins), [smem, hbm]
        out_shape = out_shape + [
            jax.ShapeDtypeStruct((256, rows), jnp.bfloat16),
            jax.ShapeDtypeStruct((32, half), jnp.bfloat16),
        ]
        out_specs = [vmem] * 6
        scratch = [
            pltpu.SMEM(freq_bins.shape, jnp.int32),
            pltpu.VMEM((32, 2 * half), jnp.float32),
            pltpu.SemaphoreType.DMA,
        ] + scratch
    else:
        kernel, operands, in_specs = fourier_kernel, (me, band, edge), [smem, vmem, vmem]
        out_shape = out_shape + [jax.ShapeDtypeStruct((1,), jnp.int32)]
        out_specs = [vmem] * 4 + [smem]
    return pl.pallas_call(
        functools.partial(kernel, parts=parts),
        in_specs=in_specs + [hbm] * 2,
        out_specs=out_specs,
        out_shape=out_shape,
        scratch_shapes=scratch,
        compiler_params=pltpu.CompilerParams(vmem_limit_bytes=48 * 2**20),
        cost_estimate=pl.CostEstimate(
            flops=COST * width, bytes_accessed=COST * width, transcendentals=0
        ),
        name="fourier",
    )(*operands, snapshots, tail)


def gram_kernel(me_ref, weight_ref, *refs, runs):
    parts, refs = refs[:4], refs[4:]
    total_in = refs[0] if len(refs) == 4 else None
    total_ref, side_ref, total = refs[-3:]
    me = me_ref[0]
    for at, comp, column, size in runs:
        here = slice(at, at + size)
        last = lax.broadcasted_iota(jnp.int32, (8, size), 0) == 7
        weight = weight_ref[comp : comp + 1, column : column + size]
        for peer in range(4):
            group = lax.rem(me - peer + 4, 4)
            rows = parts[peer][:64, here].astype(jnp.float32)
            edge = parts[(peer - 1) % 4][64:72, here].astype(jnp.float32)
            blocks = [
                rows[8 * k : 8 * k + 8] + jnp.where(last, edge[k : k + 1], 0.0) for k in range(8)
            ]
            for freq in range(4):
                both = jnp.concatenate(blocks[2 * freq : 2 * freq + 2], axis=0)
                start = pl.multiple_of(64 * freq + 16 * group, 16)
                side_ref[pl.ds(start, 16), here] = both.astype(jnp.bfloat16)
        side = side_ref[:, here]
        scaled = side.astype(jnp.float32) * weight
        high = scaled.astype(jnp.bfloat16)
        low = (scaled - high.astype(jnp.float32)).astype(jnp.bfloat16)
        dims = (((1,), (1,)), ((), ()))
        added = lax.dot_general(
            high, side, dims, preferred_element_type=jnp.float32
        ) + lax.dot_general(low, side, dims, preferred_element_type=jnp.float32)
        total[...] = added if at == 0 else total[...] + added
    lane = lax.broadcasted_iota(jnp.int32, (8, 128), 1)
    real_lane = lax.rem(lane, 16) < 8
    low_lane = lane < 64
    for pair in range(2):
        for group in range(4):
            tops = []
            for freq in (2 * pair, 2 * pair + 1):
                start = 64 * freq + 16 * group
                columns = slice(128 * pair, 128 * pair + 128)
                real = total[start : start + 8, columns]
                imag = total[start + 8 : start + 16, columns]
                turned = jnp.where(real_lane, pltpu.roll(imag, 120, 1), -pltpu.roll(imag, 8, 1))
                tops.append(real + turned)
            rows = slice(32 * pair + 8 * group, 32 * pair + 8 * group + 8)
            top = jnp.where(low_lane, tops[0], tops[1])
            total_ref[rows, :] = top if total_in is None else top + total_in[rows, :]


def gram(me, weight, parts, before, start, width):
    vmem = pl.BlockSpec(memory_space=pltpu.VMEM)
    return pl.pallas_call(
        functools.partial(gram_kernel, runs=pieces(start, width, weight.shape[1], TILE)),
        in_specs=[pl.BlockSpec(memory_space=pltpu.SMEM)] + [vmem] * (5 + len(before)),
        out_specs=[vmem] * 2,
        out_shape=[
            jax.ShapeDtypeStruct((64, 128), jnp.float32),
            jax.ShapeDtypeStruct((256, width), jnp.bfloat16),
        ],
        scratch_shapes=[pltpu.VMEM((256, 256), jnp.float32)],
        compiler_params=pltpu.CompilerParams(vmem_limit_bytes=32 * 2**20),
        cost_estimate=pl.CostEstimate(
            flops=COST * width, bytes_accessed=COST * width, transcendentals=0
        ),
        name="gram",
    )(me, weight, *parts, *before)


def split(value):
    high = value.astype(jnp.bfloat16).astype(jnp.float32)
    rest = value - high
    mid = rest.astype(jnp.bfloat16).astype(jnp.float32)
    return high, mid, rest - mid


def projections(total_ref, proj_ref):
    shape = (2, 8, 128)
    lane = lax.broadcasted_iota(jnp.int32, shape, 2)
    row = lax.broadcasted_iota(jnp.int32, shape, 1)
    real_lane = lax.rem(lane, 16) < 8
    low_lane = lane < 64
    low_row = row < 4
    place = lax.rem(row, 4)

    def turn(value):
        return jnp.where(real_lane, -pltpu.roll(value, 120, 2), pltpu.roll(value, 8, 2))

    def pick(value, j):
        return jnp.where(low_row, value[:, j : j + 1], value[:, 4 + j : 5 + j])

    def orthonormal(base):
        other = turn(base)
        for j in range(MODES):
            one, two = pick(base, j), pick(other, j)
            along = jnp.sum(base * one, axis=2, keepdims=True)
            across = jnp.sum(base * two, axis=2, keepdims=True)
            scale = lax.rsqrt(pick(along, j))
            a, b = along * scale * scale, across * scale * scale
            later = place > j
            new_base = jnp.where(later, base - a * one - b * two, base)
            new_other = jnp.where(later, other - a * two + b * one, other)
            here = place == j
            base = jnp.where(here, base * scale, new_base)
            other = jnp.where(here, other * scale, new_other)
        return base, other

    def wide(left, right):
        return jnp.concatenate([left, right], axis=1)

    groups = [
        jnp.stack([total_ref[32 * pair + 8 * g : 32 * pair + 8 * g + 8, :] for pair in range(2)])
        for g in range(4)
    ]
    rows = []
    for keep in (low_lane, jnp.logical_not(low_lane)):
        for group in groups:
            top = jnp.where(keep, group, 0.0)
            rows += [top, turn(top)]
    operators = []
    for pair in range(2):
        high, mid, low = split(jnp.concatenate([value[pair] for value in rows], axis=0))
        operators.append(
            jnp.concatenate([wide(high, low), wide(mid, jnp.zeros_like(mid))], axis=0).astype(
                jnp.bfloat16
            )
        )
    first = groups[0]
    base = jnp.where(low_row, first, pltpu.roll(first, 4, 1))
    base = jnp.where(low_row == low_lane, base, 0.0)
    base, other = orthonormal(base)
    for sweep in range(EIG_ITERS):
        high, mid, low = split(base)
        zero = jnp.zeros_like(low[0])
        results = []
        for pair in range(2):
            terms = jnp.concatenate(
                [
                    wide(high[pair], high[pair]),
                    wide(mid[pair], mid[pair]),
                    wide(low[pair], zero),
                    wide(zero, zero),
                ],
                axis=0,
            ).astype(jnp.bfloat16)
            results.append(jnp.dot(terms, operators[pair], preferred_element_type=jnp.float32))
        base = jnp.stack(
            [
                terms[:8, :128] + (terms[:8, 128:] + terms[8:16, :128] + terms[16:24, :128])
                for terms in results
            ]
        )
        base, other = orthonormal(base)
    high, mid, low = split(jnp.concatenate([base, other], axis=1))
    for pair in range(2):
        whole = lax.dot_general(
            jnp.concatenate([high[pair], high[pair], mid[pair]], axis=0).astype(jnp.bfloat16),
            jnp.concatenate([high[pair], mid[pair], high[pair]], axis=0).astype(jnp.bfloat16),
            (((0,), (0,)), ((), ())),
            preferred_element_type=jnp.float32,
        )
        ordered = []
        for freq in range(2):
            for part in range(2):
                for group in range(4):
                    start = 64 * freq + 16 * group + 8 * part
                    ordered.append(whole[start : start + 8])
        proj_ref[pair] = jnp.concatenate(ordered, axis=0).astype(jnp.bfloat16)


def recon_kernel(total_ref, *refs, runs):
    sides, (out_ref, proj_ref, held, sems) = refs[:-4], refs[-4:]
    projections(total_ref, proj_ref)
    sends = []
    for k, (side, at, comp, column, size) in enumerate(runs):
        for pair in range(2):
            result = jnp.dot(
                proj_ref[pair],
                sides[side][128 * pair : 128 * pair + 128, at : at + size],
                preferred_element_type=jnp.float32,
            ).astype(jnp.bfloat16)
            for freq in range(2):
                for part in range(2):
                    start = 64 * freq + 32 * part
                    held[2 * pair + freq, part, comp, :, column : column + size] = result[
                        start : start + 32
                    ]
        columns = pl.ds(column, size)
        send = pltpu.make_async_copy(
            held.at[:, :, comp, :, columns], out_ref.at[:, :, comp, :, columns], sems.at[k]
        )
        send.start()
        sends.append(send)
    for send in sends:
        send.wait()


def recon(total, sides, comps, points):
    runs = []
    start = 0
    for k, side in enumerate(sides):
        width = side.shape[1]
        runs += [(k, *piece) for piece in pieces(start, width, points, 2 * TILE)]
        start += width
    shape = (4, 2, comps, 32, points)
    return pl.pallas_call(
        functools.partial(recon_kernel, runs=runs),
        in_specs=[pl.BlockSpec(memory_space=pltpu.VMEM)] * (1 + len(sides)),
        out_specs=pl.BlockSpec(memory_space=pl.ANY),
        out_shape=jax.ShapeDtypeStruct(shape, jnp.bfloat16),
        scratch_shapes=[
            pltpu.VMEM((2, 128, 128), jnp.bfloat16),
            pltpu.VMEM(shape, jnp.bfloat16),
            pltpu.SemaphoreType.DMA((len(runs),)),
        ],
        compiler_params=pltpu.CompilerParams(vmem_limit_bytes=32 * 2**20),
        name="recon",
    )(total, *sides)


def point_sum(value):
    def index(y, z, core):
        return y * 8 + z * 2 + core

    partners = (
        lambda y, z, core: (y, z, 1 - core),
        lambda y, z, core: (y, z ^ 1, 1 - core),
        lambda y, z, core: (y, 3 - z, 1 - core),
        lambda y, z, core: (y ^ 1, z, 1 - core),
        lambda y, z, core: (3 - y, z, 1 - core),
    )
    for partner in partners:
        pairs = [
            (index(y, z, core), index(*partner(y, z, core)))
            for y in range(4)
            for z in range(4)
            for core in range(2)
        ]
        value = value + lax.ppermute(value, "pts", pairs)
    return value


def on_device(snapshots, tail_rows, point_weight, freq_bins):
    _, comps, points = snapshots.shape
    snapshots = jnp.transpose(snapshots, (1, 0, 2))
    tail = jnp.transpose(tail_rows, (1, 0, 2))
    me = lax.axis_index("blk").astype(jnp.int32).reshape(1)
    band = edge = None
    token = me
    arrived = []
    start = 0
    for width in CHUNKS:
        result = fourier(token, freq_bins, band, edge, snapshots, tail, start, width)
        sent = result[:4]
        if band is None:
            band, edge = result[4:]
        else:
            token = result[4]
        parts = [sent[0]]
        for shift in (1, 3, 2):
            pairs = [(k, (k + shift) % 4) for k in range(4)]
            parts.append(lax.ppermute(sent[shift], "blk", pairs))
        arrived.append((start, width, [parts[k] for k in (0, 1, 3, 2)]))
        start += width
    before = ()
    sides = []
    for start, width, parts in arrived:
        total, side = gram(me, point_weight, parts, before, start, width)
        before = (total,)
        sides.append(side)
    out = recon(point_sum(total), sides, comps, points)
    return jnp.transpose(out, (0, 1, 3, 2, 4))


def solution(mesh):
    in_specs = (P("blk", None, "pts"), P(None, None, "pts"), P(None, "pts"), P())
    out_specs = P("blk", None, None, None, "pts")
    return jax.shard_map(
        on_device, mesh=mesh, in_specs=in_specs, out_specs=out_specs, check_vma=False
    )
```

```python
import functools
import math

import jax
import jax.numpy as jnp
from jax import lax
from jax.experimental import pallas as pl
from jax.experimental.pallas import tpu as pltpu
from jax.sharding import PartitionSpec as P

MODES = 4
EIG_ITERS = 3
TILE = 512
CHUNKS = (1792, 1792, 1792, 768)
COST = 1000000


def pieces(start, width, points, most):
    result = []
    at = 0
    while at < width:
        column = (start + at) % points
        size = min(most, width - at, points - column)
        result.append((at, (start + at) // points, column, size))
        at += size
    return result


def band_kernel(me_ref, freq_ref, x_ref, tail_ref, *refs, parts):
    outs, refs = refs[:4], refs[4:]
    band_ref, edge_ref, freqs, table_ref, freq_sem = refs[:5]
    fetches = start_fetches(me_ref, x_ref, tail_ref, refs[5:], parts)
    fetch = pltpu.make_async_copy(freq_ref, freqs, freq_sem)
    fetch.start()
    fetch.wait()
    me = me_ref[0]
    half = edge_ref.shape[1]
    length = 2 * half
    row = lax.broadcasted_iota(jnp.int32, (32, length), 0)
    steps = lax.broadcasted_iota(jnp.int32, (32, length), 1)
    bins = jnp.zeros((32, length), jnp.int32)
    for k in range(16):
        bins = jnp.where(row // 2 == k, freqs[lax.rem(4 * me + k, 16)], bins)
    turns = (bins * steps + (length // 4) * lax.rem(row, 2)) & (length - 1)
    window = 0.5 - 0.5 * jnp.cos(steps[:1].astype(jnp.float32) * (2.0 * math.pi / length))
    table = window * jnp.cos(turns.astype(jnp.float32) * (2.0 * math.pi / length))
    table_ref[...] = table
    edge_ref[...] = table[:, half:].astype(jnp.bfloat16)
    block = lax.broadcasted_iota(jnp.int32, (8, half), 0)
    for r in range(0, 32, 2):
        for part in range(8):
            rows = []
            for one in (r, r + 1):
                value = jnp.where(block == part, table_ref[one : one + 1, :half], 0.0)
                rows.append(jnp.where(block == part - 1, table_ref[one : one + 1, half:], value))
            band_ref[8 * r : 8 * r + 16, half * part : half * part + half] = jnp.concatenate(
                rows, axis=0
            ).astype(jnp.bfloat16)
    transform(me_ref, band_ref, edge_ref, outs, refs[5:], parts, fetches)


def fourier_kernel(me_ref, band_ref, edge_ref, x_ref, tail_ref, *refs, parts):
    outs, refs = refs[:4], refs[4:]
    fetches = start_fetches(me_ref, x_ref, tail_ref, refs[1:], parts)
    refs[0][0] = me_ref[0]
    transform(me_ref, band_ref, edge_ref, outs, refs[1:], parts, fetches)


def start_fetches(me_ref, x_ref, tail_ref, scratch, parts):
    held, tails, sems, tail_sems = scratch
    fetches = []
    for k, (at, comp, column, size) in enumerate(parts):
        source, here = pl.ds(column, size), pl.ds(at, size)
        fetches.append(
            (
                pltpu.make_async_copy(x_ref.at[comp, :, source], held.at[:, here], sems.at[k]),
                pltpu.make_async_copy(
                    tail_ref.at[comp, :, source], tails.at[:, here], tail_sems.at[k]
                ),
            )
        )
    for fetch, _ in fetches:
        fetch.start()

    @pl.when(me_ref[0] == 0)
    def _():
        for _, fetch_tail in fetches:
            fetch_tail.start()

    return fetches


def transform(me_ref, band_ref, edge_ref, outs, scratch, parts, fetches):
    held, tails = scratch[:2]
    half = tails.shape[0]

    def edge(rows, here):
        result = jnp.dot(edge_ref[...], rows, preferred_element_type=jnp.float32)
        result = result.astype(jnp.bfloat16)
        for peer, out in enumerate(outs):
            out[64:, here] = result[8 * peer : 8 * peer + 8]

    for (at, _, _, size), (fetch, fetch_tail) in zip(parts, fetches):
        here = slice(at, at + size)
        fetch.wait()
        main = jnp.dot(band_ref[...], held[:, here], preferred_element_type=jnp.float32)
        main = main.astype(jnp.bfloat16)
        for peer, out in enumerate(outs):
            out[:64, here] = main[64 * peer : 64 * peer + 64]

        @pl.when(me_ref[0] == 0)
        def _():
            fetch_tail.wait()
            edge(tails[:, here], here)

        @pl.when(me_ref[0] != 0)
        def _():
            edge(held[:half, here], here)


def fourier(me, freq_bins, band, edge, snapshots, tail, start, width):
    comps, rows, points = snapshots.shape
    half = tail.shape[1]
    parts = pieces(start, width, points, TILE)
    vmem = pl.BlockSpec(memory_space=pltpu.VMEM)
    smem = pl.BlockSpec(memory_space=pltpu.SMEM)
    hbm = pl.BlockSpec(memory_space=pltpu.HBM)
    out_shape = [jax.ShapeDtypeStruct((72, width), jnp.bfloat16)] * 4
    scratch = [
        pltpu.VMEM((rows, width), jnp.bfloat16),
        pltpu.VMEM((half, width), jnp.bfloat16),
        pltpu.SemaphoreType.DMA((len(parts),)),
        pltpu.SemaphoreType.DMA((len(parts),)),
    ]
    if band is None:
        kernel, operands, in_specs = band_kernel, (me, freq_bins), [smem, hbm]
        out_shape = out_shape + [
            jax.ShapeDtypeStruct((256, rows), jnp.bfloat16),
            jax.ShapeDtypeStruct((32, half), jnp.bfloat16),
        ]
        out_specs = [vmem] * 6
        scratch = [
            pltpu.SMEM(freq_bins.shape, jnp.int32),
            pltpu.VMEM((32, 2 * half), jnp.float32),
            pltpu.SemaphoreType.DMA,
        ] + scratch
    else:
        kernel, operands, in_specs = fourier_kernel, (me, band, edge), [smem, vmem, vmem]
        out_shape = out_shape + [jax.ShapeDtypeStruct((1,), jnp.int32)]
        out_specs = [vmem] * 4 + [smem]
    return pl.pallas_call(
        functools.partial(kernel, parts=parts),
        in_specs=in_specs + [hbm] * 2,
        out_specs=out_specs,
        out_shape=out_shape,
        scratch_shapes=scratch,
        compiler_params=pltpu.CompilerParams(vmem_limit_bytes=48 * 2**20),
        cost_estimate=pl.CostEstimate(
            flops=COST * width, bytes_accessed=COST * width, transcendentals=0
        ),
        name="fourier",
    )(*operands, snapshots, tail)


def gram_kernel(me_ref, weight_ref, *refs, runs):
    parts, refs = refs[:4], refs[4:]
    total_in = refs[0] if len(refs) == 4 else None
    total_ref, side_ref, total = refs[-3:]
    me = me_ref[0]
    for at, comp, column, size in runs:
        here = slice(at, at + size)
        last = lax.broadcasted_iota(jnp.int32, (8, size), 0) == 7
        weight = weight_ref[comp : comp + 1, column : column + size]
        for peer in range(4):
            group = lax.rem(me - peer + 4, 4)
            rows = parts[peer][:64, here].astype(jnp.float32)
            edge = parts[(peer - 1) % 4][64:72, here].astype(jnp.float32)
            blocks = [
                rows[8 * k : 8 * k + 8] + jnp.where(last, edge[k : k + 1], 0.0) for k in range(8)
            ]
            for freq in range(4):
                both = jnp.concatenate(blocks[2 * freq : 2 * freq + 2], axis=0)
                start = pl.multiple_of(64 * freq + 16 * group, 16)
                side_ref[pl.ds(start, 16), here] = both.astype(jnp.bfloat16)
        side = side_ref[:, here]
        scaled = side.astype(jnp.float32) * weight
        high = scaled.astype(jnp.bfloat16)
        low = (scaled - high.astype(jnp.float32)).astype(jnp.bfloat16)
        dims = (((1,), (1,)), ((), ()))
        added = lax.dot_general(
            high, side, dims, preferred_element_type=jnp.float32
        ) + lax.dot_general(low, side, dims, preferred_element_type=jnp.float32)
        total[...] = added if at == 0 else total[...] + added
    lane = lax.broadcasted_iota(jnp.int32, (8, 128), 1)
    real_lane = lax.rem(lane, 16) < 8
    low_lane = lane < 64
    for pair in range(2):
        for group in range(4):
            tops = []
            for freq in (2 * pair, 2 * pair + 1):
                start = 64 * freq + 16 * group
                columns = slice(128 * pair, 128 * pair + 128)
                real = total[start : start + 8, columns]
                imag = total[start + 8 : start + 16, columns]
                turned = jnp.where(real_lane, pltpu.roll(imag, 120, 1), -pltpu.roll(imag, 8, 1))
                tops.append(real + turned)
            rows = slice(32 * pair + 8 * group, 32 * pair + 8 * group + 8)
            top = jnp.where(low_lane, tops[0], tops[1])
            total_ref[rows, :] = top if total_in is None else top + total_in[rows, :]


def gram(me, weight, parts, before, start, width):
    vmem = pl.BlockSpec(memory_space=pltpu.VMEM)
    return pl.pallas_call(
        functools.partial(gram_kernel, runs=pieces(start, width, weight.shape[1], TILE)),
        in_specs=[pl.BlockSpec(memory_space=pltpu.SMEM)] + [vmem] * (5 + len(before)),
        out_specs=[vmem] * 2,
        out_shape=[
            jax.ShapeDtypeStruct((64, 128), jnp.float32),
            jax.ShapeDtypeStruct((256, width), jnp.bfloat16),
        ],
        scratch_shapes=[pltpu.VMEM((256, 256), jnp.float32)],
        compiler_params=pltpu.CompilerParams(vmem_limit_bytes=32 * 2**20),
        cost_estimate=pl.CostEstimate(
            flops=COST * width, bytes_accessed=COST * width, transcendentals=0
        ),
        name="gram",
    )(me, weight, *parts, *before)


def split(value):
    high = value.astype(jnp.bfloat16).astype(jnp.float32)
    rest = value - high
    mid = rest.astype(jnp.bfloat16).astype(jnp.float32)
    return high, mid, rest - mid


def projections(total_ref, proj_ref):
    shape = (2, 8, 128)
    lane = lax.broadcasted_iota(jnp.int32, shape, 2)
    row = lax.broadcasted_iota(jnp.int32, shape, 1)
    real_lane = lax.rem(lane, 16) < 8
    low_lane = lane < 64
    low_row = row < 4
    place = lax.rem(row, 4)

    def turn(value):
        return jnp.where(real_lane, -pltpu.roll(value, 120, 2), pltpu.roll(value, 8, 2))

    def pick(value, j):
        return jnp.where(low_row, value[:, j : j + 1], value[:, 4 + j : 5 + j])

    def orthonormal(base):
        other = turn(base)
        along, across = [], []
        for k in range(MODES):
            for vectors, result in ((base, along), (other, across)):
                inner = jnp.sum(base * pick(vectors, k), axis=2, keepdims=True)
                result.append(jnp.broadcast_to(inner, shape))
        for j in range(MODES):
            scale = lax.rsqrt(pick(along[j], j))
            square = scale * scale
            a, b = along[j] * square, across[j] * square
            for k in range(j + 1, MODES):
                a_k, b_k = pick(a, k), pick(b, k)
                along[k], across[k] = (
                    along[k] - a_k * along[j] - b_k * across[j],
                    across[k] - a_k * across[j] + b_k * along[j],
                )
            one, two = pick(base, j), pick(other, j)
            later, here = place > j, place == j
            base, other = (
                jnp.where(later, base - a * one - b * two, jnp.where(here, base * scale, base)),
                jnp.where(later, other - a * two + b * one, jnp.where(here, other * scale, other)),
            )
        return base, other

    def wide(left, right):
        return jnp.concatenate([left, right], axis=1)

    groups = [
        jnp.stack([total_ref[32 * pair + 8 * g : 32 * pair + 8 * g + 8, :] for pair in range(2)])
        for g in range(4)
    ]
    rows = []
    for keep in (low_lane, jnp.logical_not(low_lane)):
        for group in groups:
            top = jnp.where(keep, group, 0.0)
            rows += [top, turn(top)]
    operators = []
    for pair in range(2):
        high, mid, low = split(jnp.concatenate([value[pair] for value in rows], axis=0))
        operators.append(
            jnp.concatenate([wide(high, low), wide(mid, jnp.zeros_like(mid))], axis=0).astype(
                jnp.bfloat16
            )
        )
    first = groups[0]
    base = jnp.where(low_row, first, pltpu.roll(first, 4, 1))
    base = jnp.where(low_row == low_lane, base, 0.0)
    base, other = orthonormal(base)
    for sweep in range(EIG_ITERS):
        high, mid, low = split(base)
        zero = jnp.zeros_like(low[0])
        results = []
        for pair in range(2):
            terms = jnp.concatenate(
                [
                    wide(high[pair], high[pair]),
                    wide(mid[pair], mid[pair]),
                    wide(low[pair], zero),
                    wide(zero, zero),
                ],
                axis=0,
            ).astype(jnp.bfloat16)
            results.append(jnp.dot(terms, operators[pair], preferred_element_type=jnp.float32))
        base = jnp.stack(
            [
                terms[:8, :128] + (terms[:8, 128:] + terms[8:16, :128] + terms[16:24, :128])
                for terms in results
            ]
        )
        base, other = orthonormal(base)
    high, mid, low = split(jnp.concatenate([base, other], axis=1))
    for pair in range(2):
        whole = lax.dot_general(
            jnp.concatenate([high[pair], high[pair], mid[pair]], axis=0).astype(jnp.bfloat16),
            jnp.concatenate([high[pair], mid[pair], high[pair]], axis=0).astype(jnp.bfloat16),
            (((0,), (0,)), ((), ())),
            preferred_element_type=jnp.float32,
        )
        ordered = []
        for freq in range(2):
            for part in range(2):
                for group in range(4):
                    start = 64 * freq + 16 * group + 8 * part
                    ordered.append(whole[start : start + 8])
        proj_ref[pair] = jnp.concatenate(ordered, axis=0).astype(jnp.bfloat16)


def recon_kernel(total_ref, *refs, runs):
    sides, (out_ref, proj_ref, held, sems) = refs[:-4], refs[-4:]
    projections(total_ref, proj_ref)
    sends = []
    for comp in range(out_ref.shape[2]):
        for pair in range(2):
            freqs = slice(2 * pair, 2 * pair + 2)
            for side, at, own_comp, column, size in runs:
                if own_comp != comp:
                    continue
                result = jnp.dot(
                    proj_ref[pair],
                    sides[side][128 * pair : 128 * pair + 128, at : at + size],
                    preferred_element_type=jnp.float32,
                ).astype(jnp.bfloat16)
                for freq in range(2):
                    for part in range(2):
                        start = 64 * freq + 32 * part
                        held[2 * pair + freq, part, comp, :, column : column + size] = result[
                            start : start + 32
                        ]
            send = pltpu.make_async_copy(
                held.at[freqs, :, comp], out_ref.at[freqs, :, comp], sems.at[comp, pair]
            )
            send.start()
            sends.append(send)
    for send in sends:
        send.wait()


def recon(total, sides, comps, points):
    runs = []
    start = 0
    for k, side in enumerate(sides):
        width = side.shape[1]
        runs += [(k, *piece) for piece in pieces(start, width, points, 2 * TILE)]
        start += width
    shape = (4, 2, comps, 32, points)
    return pl.pallas_call(
        functools.partial(recon_kernel, runs=runs),
        in_specs=[pl.BlockSpec(memory_space=pltpu.VMEM)] * (1 + len(sides)),
        out_specs=pl.BlockSpec(memory_space=pl.ANY),
        out_shape=jax.ShapeDtypeStruct(shape, jnp.bfloat16),
        scratch_shapes=[
            pltpu.VMEM((2, 128, 128), jnp.bfloat16),
            pltpu.VMEM(shape, jnp.bfloat16),
            pltpu.SemaphoreType.DMA((comps, 2)),
        ],
        compiler_params=pltpu.CompilerParams(vmem_limit_bytes=32 * 2**20),
        name="recon",
    )(total, *sides)


def point_sum(value):
    def index(y, z, core):
        return y * 8 + z * 2 + core

    partners = (
        lambda y, z, core: (y, z, 1 - core),
        lambda y, z, core: (y, z ^ 1, 1 - core),
        lambda y, z, core: (y, 3 - z, 1 - core),
        lambda y, z, core: (y ^ 1, z, 1 - core),
        lambda y, z, core: (3 - y, z, 1 - core),
    )
    for partner in partners:
        pairs = [
            (index(y, z, core), index(*partner(y, z, core)))
            for y in range(4)
            for z in range(4)
            for core in range(2)
        ]
        value = value + lax.ppermute(value, "pts", pairs)
    return value


def on_device(snapshots, tail_rows, point_weight, freq_bins):
    _, comps, points = snapshots.shape
    snapshots = jnp.transpose(snapshots, (1, 0, 2))
    tail = jnp.transpose(tail_rows, (1, 0, 2))
    snapshots, tail, freq_bins = (
        pltpu.with_memory_space_constraint(array, pltpu.HBM)
        for array in (snapshots, tail, freq_bins)
    )
    me = lax.axis_index("blk").astype(jnp.int32).reshape(1)
    band = edge = None
    token = me
    arrived = []
    start = 0
    for width in CHUNKS:
        result = fourier(token, freq_bins, band, edge, snapshots, tail, start, width)
        sent = result[:4]
        if band is None:
            band, edge = result[4:]
        else:
            token = result[4]
        parts = [sent[0]]
        for shift in (1, 3, 2):
            pairs = [(k, (k + shift) % 4) for k in range(4)]
            parts.append(lax.ppermute(sent[shift], "blk", pairs))
        arrived.append((start, width, [parts[k] for k in (0, 1, 3, 2)]))
        start += width
    before = ()
    sides = []
    for start, width, parts in arrived:
        total, side = gram(me, point_weight, parts, before, start, width)
        before = (total,)
        sides.append(side)
    out = recon(point_sum(total), sides, comps, points)
    return jnp.transpose(out, (0, 1, 3, 2, 4))


def solution(mesh):
    in_specs = (P("blk", None, "pts"), P(None, None, "pts"), P(None, "pts"), P())
    out_specs = P("blk", None, None, None, "pts")
    return jax.shard_map(
        on_device, mesh=mesh, in_specs=in_specs, out_specs=out_specs, check_vma=False
    )
```

```python
import functools
import math

import jax
import jax.numpy as jnp
from jax import lax
from jax.experimental import pallas as pl
from jax.experimental.pallas import tpu as pltpu
from jax.sharding import PartitionSpec as P

MODES = 4
EIG_ITERS = 3
TILE = 512
CHUNKS = (1792, 1792, 1792, 768)
COST = 1000000


def pieces(start, width, points, most):
    result = []
    at = 0
    while at < width:
        column = (start + at) % points
        size = min(most, width - at, points - column)
        result.append((at, (start + at) // points, column, size))
        at += size
    return result


def band_kernel(me_ref, freq_ref, x_ref, tail_ref, *refs, parts):
    outs, refs = refs[:4], refs[4:]
    band_ref, edge_ref, freqs, table_ref, freq_sem = refs[:5]
    fetches = start_fetches(me_ref, x_ref, tail_ref, refs[5:], parts)
    fetch = pltpu.make_async_copy(freq_ref, freqs, freq_sem)
    fetch.start()
    fetch.wait()
    me = me_ref[0]
    half = edge_ref.shape[1]
    length = 2 * half
    row = lax.broadcasted_iota(jnp.int32, (32, length), 0)
    steps = lax.broadcasted_iota(jnp.int32, (32, length), 1)
    bins = jnp.zeros((32, length), jnp.int32)
    for k in range(16):
        bins = jnp.where(row // 2 == k, freqs[lax.rem(4 * me + k, 16)], bins)
    turns = (bins * steps + (length // 4) * lax.rem(row, 2)) & (length - 1)
    window = 0.5 - 0.5 * jnp.cos(steps[:1].astype(jnp.float32) * (2.0 * math.pi / length))
    table = window * jnp.cos(turns.astype(jnp.float32) * (2.0 * math.pi / length))
    table_ref[...] = table
    edge_ref[...] = table[:, half:].astype(jnp.bfloat16)
    block = lax.broadcasted_iota(jnp.int32, (8, half), 0)
    for r in range(0, 32, 2):
        for part in range(8):
            rows = []
            for one in (r, r + 1):
                value = jnp.where(block == part, table_ref[one : one + 1, :half], 0.0)
                rows.append(jnp.where(block == part - 1, table_ref[one : one + 1, half:], value))
            band_ref[8 * r : 8 * r + 16, half * part : half * part + half] = jnp.concatenate(
                rows, axis=0
            ).astype(jnp.bfloat16)
    transform(me_ref, band_ref, edge_ref, outs, refs[5:], parts, fetches)


def fourier_kernel(me_ref, band_ref, edge_ref, x_ref, tail_ref, *refs, parts):
    outs, refs = refs[:4], refs[4:]
    fetches = start_fetches(me_ref, x_ref, tail_ref, refs[1:], parts)
    refs[0][0] = me_ref[0]
    transform(me_ref, band_ref, edge_ref, outs, refs[1:], parts, fetches)


def start_fetches(me_ref, x_ref, tail_ref, scratch, parts):
    held, tails, sems, tail_sems = scratch
    fetches = []
    for k, (at, comp, column, size) in enumerate(parts):
        source, here = pl.ds(column, size), pl.ds(at, size)
        fetches.append(
            (
                pltpu.make_async_copy(x_ref.at[comp, :, source], held.at[:, here], sems.at[k]),
                pltpu.make_async_copy(
                    tail_ref.at[comp, :, source], tails.at[:, here], tail_sems.at[k]
                ),
            )
        )
    for fetch, _ in fetches:
        fetch.start()

    @pl.when(me_ref[0] == 0)
    def _():
        for _, fetch_tail in fetches:
            fetch_tail.start()

    return fetches


def transform(me_ref, band_ref, edge_ref, outs, scratch, parts, fetches):
    held, tails = scratch[:2]
    half = tails.shape[0]

    def edge(rows, here):
        result = jnp.dot(edge_ref[...], rows, preferred_element_type=jnp.float32)
        result = result.astype(jnp.bfloat16)
        for peer, out in enumerate(outs):
            out[64:, here] = result[8 * peer : 8 * peer + 8]

    for (at, _, _, size), (fetch, fetch_tail) in zip(parts, fetches):
        here = slice(at, at + size)
        fetch.wait()
        main = jnp.dot(band_ref[...], held[:, here], preferred_element_type=jnp.float32)
        main = main.astype(jnp.bfloat16)
        for peer, out in enumerate(outs):
            out[:64, here] = main[64 * peer : 64 * peer + 64]

        @pl.when(me_ref[0] == 0)
        def _():
            fetch_tail.wait()
            edge(tails[:, here], here)

        @pl.when(me_ref[0] != 0)
        def _():
            edge(held[:half, here], here)


def fourier(me, freq_bins, band, edge, snapshots, tail, start, width):
    comps, rows, points = snapshots.shape
    half = tail.shape[1]
    parts = pieces(start, width, points, TILE)
    if band is None and width % TILE:
        first = width % TILE
        parts = [(0, 0, 0, first)] + [
            (at + first, comp, column + first, size)
            for at, comp, column, size in pieces(start, width - first, points, TILE)
        ]
    vmem = pl.BlockSpec(memory_space=pltpu.VMEM)
    smem = pl.BlockSpec(memory_space=pltpu.SMEM)
    hbm = pl.BlockSpec(memory_space=pltpu.HBM)
    out_shape = [jax.ShapeDtypeStruct((72, width), jnp.bfloat16)] * 4
    scratch = [
        pltpu.VMEM((rows, width), jnp.bfloat16),
        pltpu.VMEM((half, width), jnp.bfloat16),
        pltpu.SemaphoreType.DMA((len(parts),)),
        pltpu.SemaphoreType.DMA((len(parts),)),
    ]
    if band is None:
        kernel, operands, in_specs = band_kernel, (me, freq_bins), [smem, hbm]
        out_shape = out_shape + [
            jax.ShapeDtypeStruct((256, rows), jnp.bfloat16),
            jax.ShapeDtypeStruct((32, half), jnp.bfloat16),
        ]
        out_specs = [vmem] * 6
        scratch = [
            pltpu.SMEM(freq_bins.shape, jnp.int32),
            pltpu.VMEM((32, 2 * half), jnp.float32),
            pltpu.SemaphoreType.DMA,
        ] + scratch
    else:
        kernel, operands, in_specs = fourier_kernel, (me, band, edge), [smem, vmem, vmem]
        out_shape = out_shape + [jax.ShapeDtypeStruct((1,), jnp.int32)]
        out_specs = [vmem] * 4 + [smem]
    return pl.pallas_call(
        functools.partial(kernel, parts=parts),
        in_specs=in_specs + [hbm] * 2,
        out_specs=out_specs,
        out_shape=out_shape,
        scratch_shapes=scratch,
        compiler_params=pltpu.CompilerParams(vmem_limit_bytes=48 * 2**20),
        cost_estimate=pl.CostEstimate(
            flops=COST * width, bytes_accessed=COST * width, transcendentals=0
        ),
        name="fourier",
    )(*operands, snapshots, tail)


def gram_kernel(me_ref, weight_ref, *refs, runs):
    parts, refs = refs[:4], refs[4:]
    total_in = refs[0] if len(refs) == 4 else None
    total_ref, side_ref, total = refs[-3:]
    me = me_ref[0]
    for at, comp, column, size in runs:
        here = slice(at, at + size)
        last = lax.broadcasted_iota(jnp.int32, (8, size), 0) == 7
        weight = weight_ref[comp : comp + 1, column : column + size]
        for peer in range(4):
            group = lax.rem(me - peer + 4, 4)
            rows = parts[peer][:64, here].astype(jnp.float32)
            edge = parts[(peer - 1) % 4][64:72, here].astype(jnp.float32)
            blocks = [
                rows[8 * k : 8 * k + 8] + jnp.where(last, edge[k : k + 1], 0.0) for k in range(8)
            ]
            for freq in range(4):
                both = jnp.concatenate(blocks[2 * freq : 2 * freq + 2], axis=0)
                start = pl.multiple_of(64 * freq + 16 * group, 16)
                side_ref[pl.ds(start, 16), here] = both.astype(jnp.bfloat16)
        side = side_ref[:, here]
        scaled = side.astype(jnp.float32) * weight
        high = scaled.astype(jnp.bfloat16)
        low = (scaled - high.astype(jnp.float32)).astype(jnp.bfloat16)
        dims = (((1,), (1,)), ((), ()))
        added = lax.dot_general(
            high, side, dims, preferred_element_type=jnp.float32
        ) + lax.dot_general(low, side, dims, preferred_element_type=jnp.float32)
        total[...] = added if at == 0 else total[...] + added
    lane = lax.broadcasted_iota(jnp.int32, (8, 128), 1)
    real_lane = lax.rem(lane, 16) < 8
    low_lane = lane < 64
    for pair in range(2):
        for group in range(4):
            tops = []
            for freq in (2 * pair, 2 * pair + 1):
                start = 64 * freq + 16 * group
                columns = slice(128 * pair, 128 * pair + 128)
                real = total[start : start + 8, columns]
                imag = total[start + 8 : start + 16, columns]
                turned = jnp.where(real_lane, pltpu.roll(imag, 120, 1), -pltpu.roll(imag, 8, 1))
                tops.append(real + turned)
            rows = slice(32 * pair + 8 * group, 32 * pair + 8 * group + 8)
            top = jnp.where(low_lane, tops[0], tops[1])
            total_ref[rows, :] = top if total_in is None else top + total_in[rows, :]


def gram(me, weight, parts, before, start, width):
    vmem = pl.BlockSpec(memory_space=pltpu.VMEM)
    return pl.pallas_call(
        functools.partial(gram_kernel, runs=pieces(start, width, weight.shape[1], TILE)),
        in_specs=[pl.BlockSpec(memory_space=pltpu.SMEM)] + [vmem] * (5 + len(before)),
        out_specs=[vmem] * 2,
        out_shape=[
            jax.ShapeDtypeStruct((64, 128), jnp.float32),
            jax.ShapeDtypeStruct((256, width), jnp.bfloat16),
        ],
        scratch_shapes=[pltpu.VMEM((256, 256), jnp.float32)],
        compiler_params=pltpu.CompilerParams(vmem_limit_bytes=32 * 2**20),
        cost_estimate=pl.CostEstimate(
            flops=COST * width, bytes_accessed=COST * width, transcendentals=0
        ),
        name="gram",
    )(me, weight, *parts, *before)


def split(value):
    high = value.astype(jnp.bfloat16).astype(jnp.float32)
    rest = value - high
    mid = rest.astype(jnp.bfloat16).astype(jnp.float32)
    return high, mid, rest - mid


def projections(total_ref, proj_ref):
    shape = (2, 8, 128)
    lane = lax.broadcasted_iota(jnp.int32, shape, 2)
    row = lax.broadcasted_iota(jnp.int32, shape, 1)
    real_lane = lax.rem(lane, 16) < 8
    low_lane = lane < 64
    low_row = row < 4
    place = lax.rem(row, 4)

    def turn(value):
        return jnp.where(real_lane, -pltpu.roll(value, 120, 2), pltpu.roll(value, 8, 2))

    def pick(value, j):
        return jnp.where(low_row, value[:, j : j + 1], value[:, 4 + j : 5 + j])

    def orthonormal(base):
        other = turn(base)
        along, across = [], []
        for k in range(MODES):
            for vectors, result in ((base, along), (other, across)):
                inner = jnp.sum(base * pick(vectors, k), axis=2, keepdims=True)
                result.append(jnp.broadcast_to(inner, shape))
        for j in range(MODES):
            scale = lax.rsqrt(pick(along[j], j))
            square = scale * scale
            a, b = along[j] * square, across[j] * square
            for k in range(j + 1, MODES):
                a_k, b_k = pick(a, k), pick(b, k)
                along[k], across[k] = (
                    along[k] - a_k * along[j] - b_k * across[j],
                    across[k] - a_k * across[j] + b_k * along[j],
                )
            one, two = pick(base, j), pick(other, j)
            later, here = place > j, place == j
            base, other = (
                jnp.where(later, base - a * one - b * two, jnp.where(here, base * scale, base)),
                jnp.where(later, other - a * two + b * one, jnp.where(here, other * scale, other)),
            )
        return base, other

    def wide(left, right):
        return jnp.concatenate([left, right], axis=1)

    groups = [
        jnp.stack([total_ref[32 * pair + 8 * g : 32 * pair + 8 * g + 8, :] for pair in range(2)])
        for g in range(4)
    ]
    rows = []
    for keep in (low_lane, jnp.logical_not(low_lane)):
        for group in groups:
            top = jnp.where(keep, group, 0.0)
            rows += [top, turn(top)]
    operators = []
    for pair in range(2):
        high, mid, low = split(jnp.concatenate([value[pair] for value in rows], axis=0))
        operators.append(
            jnp.concatenate([wide(high, low), wide(mid, jnp.zeros_like(mid))], axis=0).astype(
                jnp.bfloat16
            )
        )
    first = groups[0]
    base = jnp.where(low_row, first, pltpu.roll(first, 4, 1))
    base = jnp.where(low_row == low_lane, base, 0.0)
    base, other = orthonormal(base)
    for sweep in range(EIG_ITERS):
        high, mid, low = split(base)
        zero = jnp.zeros_like(low[0])
        results = []
        for pair in range(2):
            terms = jnp.concatenate(
                [
                    wide(high[pair], high[pair]),
                    wide(mid[pair], mid[pair]),
                    wide(low[pair], zero),
                    wide(zero, zero),
                ],
                axis=0,
            ).astype(jnp.bfloat16)
            results.append(jnp.dot(terms, operators[pair], preferred_element_type=jnp.float32))
        base = jnp.stack(
            [
                terms[:8, :128] + (terms[:8, 128:] + terms[8:16, :128] + terms[16:24, :128])
                for terms in results
            ]
        )
        base, other = orthonormal(base)
    high, mid, low = split(jnp.concatenate([base, other], axis=1))
    for pair in range(2):
        whole = lax.dot_general(
            jnp.concatenate([high[pair], high[pair], mid[pair]], axis=0).astype(jnp.bfloat16),
            jnp.concatenate([high[pair], mid[pair], high[pair]], axis=0).astype(jnp.bfloat16),
            (((0,), (0,)), ((), ())),
            preferred_element_type=jnp.float32,
        )
        ordered = []
        for freq in range(2):
            for part in range(2):
                for group in range(4):
                    start = 64 * freq + 16 * group + 8 * part
                    ordered.append(whole[start : start + 8])
        proj_ref[pair] = jnp.concatenate(ordered, axis=0).astype(jnp.bfloat16)


def recon_kernel(total_ref, *refs, runs):
    sides, (out_ref, proj_ref, held, sems) = refs[:-4], refs[-4:]
    projections(total_ref, proj_ref)
    sends = []
    for comp in range(out_ref.shape[2]):
        for pair in range(2):
            freqs = slice(2 * pair, 2 * pair + 2)
            for side, at, own_comp, column, size in runs:
                if own_comp != comp:
                    continue
                result = jnp.dot(
                    proj_ref[pair],
                    sides[side][128 * pair : 128 * pair + 128, at : at + size],
                    preferred_element_type=jnp.float32,
                ).astype(jnp.bfloat16)
                for freq in range(2):
                    for part in range(2):
                        start = 64 * freq + 32 * part
                        held[2 * pair + freq, part, comp, :, column : column + size] = result[
                            start : start + 32
                        ]
            send = pltpu.make_async_copy(
                held.at[freqs, :, comp], out_ref.at[freqs, :, comp], sems.at[comp, pair]
            )
            send.start()
            sends.append(send)
    for send in sends:
        send.wait()


def recon(total, sides, comps, points):
    runs = []
    start = 0
    for k, side in enumerate(sides):
        width = side.shape[1]
        runs += [(k, *piece) for piece in pieces(start, width, points, 2 * TILE)]
        start += width
    shape = (4, 2, comps, 32, points)
    return pl.pallas_call(
        functools.partial(recon_kernel, runs=runs),
        in_specs=[pl.BlockSpec(memory_space=pltpu.VMEM)] * (1 + len(sides)),
        out_specs=pl.BlockSpec(memory_space=pl.ANY),
        out_shape=jax.ShapeDtypeStruct(shape, jnp.bfloat16),
        scratch_shapes=[
            pltpu.VMEM((2, 128, 128), jnp.bfloat16),
            pltpu.VMEM(shape, jnp.bfloat16),
            pltpu.SemaphoreType.DMA((comps, 2)),
        ],
        compiler_params=pltpu.CompilerParams(vmem_limit_bytes=32 * 2**20),
        name="recon",
    )(total, *sides)


def point_sum(value):
    def index(y, z, core):
        return y * 8 + z * 2 + core

    partners = (
        lambda y, z, core: (y, z, 1 - core),
        lambda y, z, core: (y, z ^ 1, 1 - core),
        lambda y, z, core: (y, 3 - z, 1 - core),
        lambda y, z, core: (y ^ 1, z, 1 - core),
        lambda y, z, core: (3 - y, z, 1 - core),
    )
    for partner in partners:
        pairs = [
            (index(y, z, core), index(*partner(y, z, core)))
            for y in range(4)
            for z in range(4)
            for core in range(2)
        ]
        value = value + lax.ppermute(value, "pts", pairs)
    return value


def on_device(snapshots, tail_rows, point_weight, freq_bins):
    _, comps, points = snapshots.shape
    snapshots = jnp.transpose(snapshots, (1, 0, 2))
    tail = jnp.transpose(tail_rows, (1, 0, 2))
    snapshots, tail, freq_bins = (
        pltpu.with_memory_space_constraint(array, pltpu.HBM)
        for array in (snapshots, tail, freq_bins)
    )
    me = lax.axis_index("blk").astype(jnp.int32).reshape(1)
    band = edge = None
    token = me
    arrived = []
    start = 0
    for width in CHUNKS:
        result = fourier(token, freq_bins, band, edge, snapshots, tail, start, width)
        sent = result[:4]
        if band is None:
            band, edge = result[4:]
        else:
            token = result[4]
        parts = [sent[0]]
        for shift in (1, 3, 2):
            pairs = [(k, (k + shift) % 4) for k in range(4)]
            parts.append(lax.ppermute(sent[shift], "blk", pairs))
        arrived.append((start, width, [parts[k] for k in (0, 1, 3, 2)]))
        start += width
    before = ()
    sides = []
    for start, width, parts in arrived:
        total, side = gram(me, point_weight, parts, before, start, width)
        before = (total,)
        sides.append(side)
    out = recon(point_sum(total), sides, comps, points)
    return jnp.transpose(out, (0, 1, 3, 2, 4))


def solution(mesh):
    in_specs = (P("blk", None, "pts"), P(None, None, "pts"), P(None, "pts"), P())
    out_specs = P("blk", None, None, None, "pts")
    return jax.shard_map(
        on_device, mesh=mesh, in_specs=in_specs, out_specs=out_specs, check_vma=False
    )
```
